32 devices in a mesh: expert: 8 (over z, x), dp: 4 (over y, core).
Axes of the slice: x: 2, y: 2, z: 4, core: 2. Of those that a mesh axis runs over, the one named last changes fastest.
Arguments:
- tokens: bfloat16 [4096, 1024], P(('expert', 'dp')), may hold values from -6 to 6
- expert_ids: int32 [4096, 2], P(('expert', 'dp')), may hold values from 0 to 7, all different within a row; in each aligned block of 128 rows (0 to 127, 128 to 255, ...) at most 48 rows name the same one
- combine: float32 [4096, 2], P(('expert', 'dp')), may hold values from 0.25 to 1
- language: int32 [4096], P(('expert', 'dp')), may hold values from 0 to 7
- lang_slot: int32 [8], replicated, may hold values from 0 to 7, each once
- up_weight: bfloat16 [8, 1024, 4096], P('expert', None, 'dp'), may hold values from -0.1875 to 0.1875
- down_weight: bfloat16 [8, 4096, 1024], P('expert', 'dp'), may hold values from -0.09375 to 0.09375
- adapter_in: bfloat16 [8, 8, 16, 4096], P('dp', 'expert'), may hold values from -0.09375 to 0.09375
- adapter_out: bfloat16 [8, 8, 16, 1024], P('dp', 'expert'), may hold values from -1.5 to 1.5
Outputs:
- mixed: bfloat16 [4096, 1024], P(('expert', 'dp'))
The draws below stay inside these ranges and needn't reach their ends.
Inputs may be any that keep to these rules, and one draw needn't show every extreme that they name: `expert_ids`: the two experts of a token differ; among the tokens of one device no expert is named by more than 48 choices, a bound that some block reaches. `lang_slot`: each slot holds exactly one language.
All inputs are finite; a program needn't handle non-finite values.
Results may differ from the reference program's by a relative error of at most 0.015.
Values may be sent and summed in bfloat16 or wider, within the bound.
No kernel may reach another device: no remote copies, remote signals or barrier semaphores. Data moves between devices by JAX's collectives and lax.ppermute only.
A program may use at most 128 MiB of HBM per device.

```python
import math
import jax
import jax.numpy as jnp
import numpy as np
from jax import lax

D = 1024
HID = 4096
R = 16
LANGS = 8
TOK_DEV = 128
EXPERTS = 8
CAP = 48
HID_DEV = 1024
TOKENS = 4096
N_EXPERT = 8
N_DP = 4


def with_ends(result, rng, low, largest):
    spot = [jax.random.randint(jax.random.fold_in(rng, axis), (), 0, length) for axis, length in enumerate(result.shape)]
    widest = result.shape.index(max(result.shape))
    next_to = spot[:widest] + [(spot[widest] + 1) % result.shape[widest]] + spot[widest + 1:]
    return result.at[tuple(spot)].set(low).at[tuple(next_to)].set(largest)


def levels(own_key, extent, pieces, least, high):
    gain = 1.0
    for position, blocks in pieces:
        draws = jax.random.uniform(jax.random.fold_in(jax.random.fold_in(own_key, 6), position), (blocks,), jnp.float32, least / len(pieces), high / len(pieces))
        gain = gain * jnp.repeat(jnp.exp(draws), extent[position] // blocks).reshape((-1,) + (1,) * (len(extent) - 1 - position))
    return gain


def rank_table(count, skew):
    weights = [(1 << 20) // math.isqrt(standing ** skew) + 1 for standing in range(1, count + 1)]
    width = 1 + sum(weights) // (1 << 30)
    return np.cumsum(np.array([max(1, weight // width) for weight in weights]))


def ranked(key, dims, amount, skew):
    table = rank_table(amount, skew)
    lot = jax.random.randint(jax.random.fold_in(key, 1), dims, 0, int(table[amount - 1]))
    rank = jnp.searchsorted(jnp.asarray(table, jnp.int32), lot, side="right")
    return jax.random.permutation(jax.random.fold_in(key, 2), amount)[rank].astype(jnp.int32)


def shared_out(key, own, number, rows, count, top, most, lean):
    order = jax.random.permutation(key, count)
    heavy_load, common = shares(count, rows * top, most, lean, True), shares(count, rows * top, most, lean, False)
    places = jnp.arange(count)

    def named(tallies, offset_by):
        used = int((tallies > 0).sum())
        fixed = max(1, used // 4)
        moved = fixed + (places - fixed + offset_by * (used - fixed)) % max(1, count - fixed)
        return jnp.zeros((count,), jnp.int32).at[order[jnp.where(places < fixed, places, moved)]].set(jnp.asarray(tallies, jnp.int32))

    tallies = jnp.where(number % 4 == 0, named(heavy_load, number // 4), named(common, number - number // 4 - 1))
    mixed = jax.random.permutation(jax.random.fold_in(own, 3), count)
    giver, sink = mixed[0:count // 2 * 2:2], mixed[1:count // 2 * 2:2]
    margin = jnp.minimum(tallies[giver] - 1, most - tallies[sink]) // 2
    margin = jnp.where((giver == order[0]) | (sink == order[0]) | (tallies[sink] == 0), 0, jnp.maximum(margin, 0))
    moved = jax.random.randint(jax.random.fold_in(own, 4), (count // 2,), 0, 1 << 20) % (margin + 1)
    tallies = tallies.at[giver].add(-moved).at[sink].add(moved)
    members = jnp.searchsorted(jnp.cumsum(tallies), jnp.arange(rows * top), side="right").astype(jnp.int32)
    table = members.reshape(top, rows).T
    table = table[jax.random.permutation(jax.random.fold_in(own, 1), rows)]
    offset_by = jax.random.randint(jax.random.fold_in(own, 2), (rows, 1), 0, top)
    return jnp.take_along_axis(table, (jnp.arange(top)[None, :] + offset_by) % top, axis=1)


def shares(count, total, most, lean, full):
    weights = [(1 << 20) // math.isqrt(grade ** lean) + 1 for grade in range(1, count + 1)]
    largest = most if full else min(most, max(-(-total // count), total * weights[0] // sum(weights)))
    least = 1 if total - largest >= count - 1 else 0
    given, spare = [largest] + [least] * (count - 1), total - largest - least * (count - 1)
    while spare > 0:
        candidates = [i for i in range(1, count) if given[i] < largest] or [i for i in range(1, count) if given[i] < most]
        mass, left = sum([weights[i] for i in candidates]), spare
        for i in candidates:
            addition = min(most - given[i], max(1, left * weights[i] // mass), spare)
            given[i] = given[i] + addition
            spare = spare - addition
    return np.array(given)


def bell_draw(own_key, dims, scale, limit, cuts=(), held_as=jnp.bfloat16):
    drawn = jax.random.normal(own_key, dims, jnp.float32) * scale
    if len(cuts) > 0:
        drawn = levels(own_key, dims, cuts, -0.22, 0.18) * drawn
    return jnp.clip(drawn, min=-limit, max=limit).astype(held_as)


def setup_inputs(seed: int = 0) -> dict:
    key_of = jax.random.split(jax.random.key(seed), 10)
    tokens = bell_draw(key_of[0], (TOKENS, D), 1.0, 6.0, ((0, 32),))
    expert_ids_keys = jax.random.split(jax.random.fold_in(key_of[1], 1), TOKENS // TOK_DEV)
    expert_ids_turns = jax.random.permutation(jax.random.fold_in(key_of[1], 3), TOKENS // TOK_DEV)
    expert_ids = jax.vmap(lambda own, number: shared_out(jax.random.fold_in(key_of[1], 2), own, number, TOK_DEV, EXPERTS, 2, CAP, 2))(expert_ids_keys, expert_ids_turns).reshape((TOKENS, 2))
    combine = jnp.clip(0.25 + 0.75 * jax.random.uniform(key_of[2], (TOKENS, 2), jnp.float32) ** levels(key_of[2], (TOKENS, 2), ((0, 32),), -0.2, 0.2), 0.25, 1.0)
    language = with_ends(ranked(key_of[3], (TOKENS,), LANGS, 2), jax.random.fold_in(key_of[3], 3), 0, LANGS - 1).astype(jnp.int32)
    lang_slot = jax.random.permutation(key_of[4], LANGS).astype(jnp.int32)
    up_weight = bell_draw(key_of[5], (EXPERTS, D, HID), D ** -0.5, 0.1875, ((0, 8), (2, 4)))
    down_weight = bell_draw(key_of[6], (EXPERTS, HID, D), HID ** -0.5, 0.09375, ((0, 8), (1, 4)))
    adapter_in = bell_draw(key_of[7], (LANGS, EXPERTS, R, HID), HID ** -0.5, 0.09375, ((0, 4), (1, 8)))
    adapter_out = bell_draw(key_of[8], (LANGS, EXPERTS, R, D), R ** -0.5, 1.5, ((0, 4), (1, 8)))
    return {"tokens": tokens, "expert_ids": expert_ids, "combine": combine, "language": language, "lang_slot": lang_slot, "up_weight": up_weight, "down_weight": down_weight, "adapter_in": adapter_in, "adapter_out": adapter_out}


def expert_part(sent_rows, slot_codes, w_up, down_matrix, adapter_input_piece, adapter_output_full):
    language_count = adapter_input_piece.shape[0]
    adapter_rank = adapter_input_piece.shape[1]
    hidden_state = jnp.maximum(jnp.dot(sent_rows, w_up, preferred_element_type=jnp.float32), 0.0).astype(jnp.bfloat16)
    input_flattened = adapter_input_piece.reshape(language_count * adapter_rank, adapter_input_piece.shape[2])
    reduced_rank = lax.dot_general(hidden_state, input_flattened, (((1,), (1,)), ((), ())), preferred_element_type=jnp.float32)
    column_position = jnp.arange(language_count * adapter_rank, dtype=jnp.int32) // adapter_rank
    keep_mask = (slot_codes[:, None] - 1) == column_position[None, :]
    reduced_rank = jnp.where(keep_mask, reduced_rank, 0.0).astype(jnp.bfloat16)
    output_flattened = adapter_output_full.reshape(language_count * adapter_rank, adapter_output_full.shape[2])
    adapter_update = jnp.dot(reduced_rank, output_flattened, preferred_element_type=jnp.float32)
    return jnp.dot(hidden_state, down_matrix, preferred_element_type=jnp.float32) + adapter_update


def reference(tokens, expert_ids, combine, language, lang_slot, up_weight, down_weight, adapter_in, adapter_out):
    tok_count = tokens.shape[0]
    model_width = tokens.shape[1]
    adapter_slot = jnp.take(lang_slot, language)
    flat_route = jnp.concatenate([expert_ids[:, 0], expert_ids[:, 1]])
    flat_token = jnp.concatenate([jnp.arange(tok_count, dtype=jnp.int32), jnp.arange(tok_count, dtype=jnp.int32)])
    flat_weight = jnp.concatenate([combine[:, 0], combine[:, 1]])
    row_limit = N_EXPERT * N_DP * CAP

    def one_expert(running, expert):
        chosen = flat_route == expert
        picked = jnp.nonzero(chosen, size=row_limit, fill_value=0)[0].astype(jnp.int32)
        is_valid = jnp.arange(row_limit, dtype=jnp.int32) < jnp.sum(chosen.astype(jnp.int32))
        token_index = jnp.take(flat_token, picked)
        sent_rows = jnp.take(tokens, token_index, axis=0)
        slot_codes = jnp.where(is_valid, jnp.take(adapter_slot, token_index) + 1, 0)
        w_up = up_weight[expert]
        down_matrix = down_weight[expert]
        in_all = adapter_in[:, expert]
        out_all = adapter_out[:, expert]
        summed = jnp.zeros((row_limit, model_width), jnp.float32)
        for group_id in range(N_DP):
            offset = group_id * HID_DEV
            partial_term = expert_part(sent_rows, slot_codes, w_up[:, offset:offset + HID_DEV],
                                       down_matrix[offset:offset + HID_DEV], in_all[:, :, offset:offset + HID_DEV], out_all)
            rounded = lax.optimization_barrier(partial_term.astype(jnp.bfloat16))
            summed = summed + rounded.astype(jnp.float32)
        expert_out = lax.optimization_barrier(summed.astype(jnp.bfloat16)).astype(jnp.float32)
        weight_row = jnp.where(is_valid, jnp.take(flat_weight, picked), 0.0)
        running = running.at[token_index].add(weight_row[:, None] * expert_out)
        return running, None

    running, unused = lax.scan(one_expert, jnp.zeros((tok_count, model_width), jnp.float32),
                               jnp.arange(N_EXPERT, dtype=jnp.int32))
    return running.astype(jnp.bfloat16)
```

```python
import functools

import jax
import jax.numpy as jnp
from jax import lax
from jax.experimental import pallas as pl
from jax.experimental.pallas import tpu as pltpu
from jax.sharding import PartitionSpec as P

F32 = jnp.float32
BF16 = jnp.bfloat16
VMEM = pl.BlockSpec(memory_space=pltpu.VMEM)
SMEM = pl.BlockSpec(memory_space=pltpu.SMEM)
ANY = pl.BlockSpec(memory_space=pl.ANY)


def iota(shape, dim):
    return lax.broadcasted_iota(jnp.int32, shape, dim)


def row_places(hit):
    count = hit.shape[1]
    earlier = (iota((count, count), 0) < iota((count, count), 1)).astype(BF16)
    place = jnp.dot(hit.astype(F32).astype(BF16), earlier, preferred_element_type=F32)
    return jnp.where(hit, place, -1.0)


def prep_kernel(cap, slot_ref, ids_ref, lang_ref, tok_ref, *outs):
    experts = len(outs) - 1
    count = tok_ref.shape[0]
    me = lax.axis_index("expert")
    first, second = ids_ref[0:1, :], ids_ref[1:2, :]
    expert = iota((experts, count), 0) ^ me
    place = row_places((first == expert) | (second == expert))
    want = iota((cap, count), 0).astype(F32)
    select = jnp.concatenate(
        [(place[j : j + 1, :] == want).astype(F32).astype(BF16) for j in range(experts)], axis=0
    )
    rows = jnp.dot(select, tok_ref[...], preferred_element_type=F32).astype(BF16)
    for j in range(experts):
        outs[j][...] = rows[j * cap : (j + 1) * cap]
    lang = lang_ref[...]
    slot = jnp.zeros_like(lang)
    for i in range(slot_ref.shape[0]):
        slot = jnp.where(lang == i, slot_ref[i], slot)
    outs[experts][...] = first + experts * second + experts * experts * slot


def row_slots(codes, cap, experts):
    me = lax.axis_index("expert")
    sources, count = codes.shape
    first = lax.rem(codes, experts)
    second = lax.rem(lax.div(codes, experts), experts)
    slot = lax.div(codes, experts * experts).astype(F32)
    place = row_places((first == me) | (second == me))
    want = iota((cap, count), 0).astype(F32)
    found = [
        jnp.sum(
            jnp.where(place[s : s + 1, :] == want, slot[s : s + 1, :] + 1.0, 0.0),
            axis=1,
            keepdims=True,
        )
        for s in range(sources)
    ]
    return jnp.concatenate(found, axis=0) - 1.0


def expert_kernel(
    cap, experts, rank, blocks, codes_ref, peer_ref, own_a_ref, own_b_ref, up_a, up_b, down_a, down_b,
    ain_ref, aout_ref, send_ref, keep_ref, up_buf, down_buf, sems,
):
    hid = up_a.shape[1]
    step = hid // blocks
    copies = []
    for h, (up, down) in enumerate(((up_a, down_a), (up_b, down_b))):
        for b in range(blocks):
            span = pl.ds(b * step, step)
            one = pltpu.make_async_copy(up.at[:, span], up_buf.at[h, :, span], sems.at[0, h, b])
            two = pltpu.make_async_copy(down.at[span, :], down_buf.at[h, span, :], sems.at[1, h, b])
            one.start()
            two.start()
            copies.append((one, two))
    dp = lax.axis_index("dp")
    slots = row_slots(codes_ref[...], cap, experts)
    width = aout_ref.shape[0]
    column = iota((1, width), 1)
    part = lax.div(column, width // 4)
    owner = dp ^ (lax.rem(part, 2) * 2 + lax.div(part, 2))
    column_slot = owner * (width // 4 // rank) + lax.rem(lax.div(column, rank), width // 4 // rank)
    keep = slots == column_slot.astype(F32)
    rows = jnp.concatenate([peer_ref[...], own_a_ref[...], own_b_ref[...]], axis=0)
    total = jnp.zeros((rows.shape[0], aout_ref.shape[1]), F32)
    core = lax.rem(dp, 2)
    for h in range(2):
        low = jnp.zeros((rows.shape[0], width), F32)
        base = (core ^ h) * hid
        for b in range(blocks):
            span = pl.ds(b * step, step)
            one, two = copies[h * blocks + b]
            one.wait()
            hidden = jnp.dot(rows, up_buf[h, :, span], preferred_element_type=F32)
            hidden = jnp.maximum(hidden, 0.0).astype(BF16)
            two.wait()
            total += jnp.dot(hidden, down_buf[h, span, :], preferred_element_type=F32)
            where = pl.ds(pl.multiple_of(base + b * step, step), step)
            low += lax.dot_general(
                hidden, ain_ref[:, where], (((1,), (1,)), ((), ())), preferred_element_type=F32
            )
        low = jnp.where(keep, low, 0.0).astype(BF16)
        total += jnp.dot(low, aout_ref[...], preferred_element_type=F32)
    half = rows.shape[0] // 2
    send_ref[...] = total[:half].astype(BF16)
    keep_ref[...] = total[half:]


def mix_kernel(cap, ids_ref, combine_ref, *refs):
    backs, out_ref = refs[:-1], refs[-1]
    experts = len(backs)
    count = ids_ref.shape[0]
    me = lax.axis_index("expert")
    first, second = ids_ref[:, 0:1] ^ me, ids_ref[:, 1:2] ^ me
    lane = iota((count, 128), 1)
    hit = ((first == lane) | (second == lane)).astype(F32).astype(BF16)
    earlier = (iota((count, count), 1) < iota((count, count), 0)).astype(F32).astype(BF16)
    place = jnp.dot(earlier, hit, preferred_element_type=F32)
    back = jnp.concatenate([b[...] for b in backs], axis=0)
    spot = iota((count, experts * cap), 1).astype(F32)
    mixed = None
    for k, choice in enumerate((first, second)):
        at = jnp.sum(jnp.where(choice == lane, place, 0.0), axis=1, keepdims=True)
        at = at + (choice * cap).astype(F32)
        select = (at == spot).astype(F32).astype(BF16)
        picked = jnp.dot(select, back, preferred_element_type=F32)
        term = combine_ref[:, k : k + 1] * picked
        mixed = term if mixed is None else mixed + term
    out_ref[...] = mixed.astype(BF16)


def flip(x, axis, bit):
    size = lax.axis_size(axis)
    return lax.ppermute(x, axis, [(i, i ^ bit) for i in range(size)])


def local_pairs(
    tokens, expert_ids, combine, language, lang_slot, up_weight, down_weight, adapter_in, adapter_out
):
    count, width = tokens.shape
    experts = lax.axis_size("expert")
    cap = 3 * count // experts
    slots, _, rank, hid_all = adapter_in.shape
    up, down = up_weight[0], down_weight[0]
    hid = up.shape[1]

    up_other, down_other = flip(up, "dp", 1), flip(down, "dp", 1)

    prep = pl.pallas_call(
        functools.partial(prep_kernel, cap),
        out_shape=[jax.ShapeDtypeStruct((cap, width), BF16)] * experts
        + [jax.ShapeDtypeStruct((1, count), jnp.int32)],
        in_specs=[SMEM, VMEM, VMEM, VMEM],
        out_specs=[VMEM] * (experts + 1),
        cost_estimate=pl.CostEstimate(flops=10**8, bytes_accessed=2 * 10**6, transcendentals=0),
        name="prep",
    )(lang_slot, expert_ids.T, language[None, :], tokens)
    send, code = prep[:experts], prep[experts]

    got = [send[0]] + [None] * (experts - 1)
    order = [j ^ 1 for j in range(experts - 1, 0, -1)]
    order = [j if j else 1 for j in order]
    for j in order:
        got[j] = flip(send[j], "expert", j)

    bit = 1
    while bit < experts:
        code = jnp.concatenate([code, flip(code, "expert", bit)], axis=0)
        bit *= 2
    code_peer = flip(code, "dp", 2)

    y = lax.axis_index("dp") // 2
    flat_in = adapter_in.reshape(slots * rank, hid_all)
    flat_out = adapter_out.reshape(slots * rank, width)
    mine = lax.dynamic_slice_in_dim(flat_in, y * 2 * hid, 2 * hid, 1)
    theirs = lax.dynamic_slice_in_dim(flat_in, (1 - y) * 2 * hid, 2 * hid, 1)
    other = flip(jnp.concatenate([theirs, flat_out], axis=1), "dp", 2)
    pair = jnp.concatenate([jnp.concatenate([mine, flat_out], axis=1), other], axis=0)
    full = jnp.concatenate([pair, flip(pair, "dp", 1)], axis=0)
    ain, aout = full[:, : 2 * hid], full[:, 2 * hid :]

    blocks = 4
    backs = [None] * experts
    for k in range(experts // 2 - 1, -1, -1):
        a, b = got[2 * k], got[2 * k + 1]
        peer = flip(jnp.concatenate([a, b], axis=0), "dp", 2)
        codes = jnp.concatenate([code_peer[2 * k : 2 * k + 2], code[2 * k : 2 * k + 2]], axis=0)
        part, own = pl.pallas_call(
            functools.partial(expert_kernel, cap, experts, rank, blocks),
            out_shape=[
                jax.ShapeDtypeStruct((2 * cap, width), BF16),
                jax.ShapeDtypeStruct((2 * cap, width), F32),
            ],
            in_specs=[VMEM, VMEM, VMEM, VMEM, ANY, ANY, ANY, ANY, VMEM, VMEM],
            out_specs=[VMEM, VMEM],
            scratch_shapes=[
                pltpu.VMEM((2, width, hid), BF16),
                pltpu.VMEM((2, hid, width), BF16),
                pltpu.SemaphoreType.DMA((2, 2, blocks)),
            ],
            compiler_params=pltpu.CompilerParams(vmem_limit_bytes=32 * 2**20),
            cost_estimate=pl.CostEstimate(
                flops=16 * cap * width * hid, bytes_accessed=10 * 2**20, transcendentals=0
            ),
            name="expert",
        )(codes, peer, a, b, up, up_other, down, down_other, ain, aout)
        done = (own + flip(part, "dp", 2).astype(F32)).astype(BF16)
        for i in range(2):
            j = 2 * k + i
            piece = done[i * cap : (i + 1) * cap]
            backs[j] = flip(piece, "expert", j) if j else piece

    return pl.pallas_call(
        functools.partial(mix_kernel, cap),
        out_shape=jax.ShapeDtypeStruct((count, width), BF16),
        in_specs=[VMEM] * (2 + experts),
        out_specs=VMEM,
        cost_estimate=pl.CostEstimate(flops=2 * 10**8, bytes_accessed=2 * 10**6, transcendentals=0),
        name="mix",
    )(expert_ids, combine, *backs)


def expert_part(sent_rows, slot_codes, w_up, down_matrix, adapter_input_piece, adapter_output_full):
    language_count = adapter_input_piece.shape[0]
    adapter_rank = adapter_input_piece.shape[1]
    hidden_state = jnp.maximum(
        jnp.dot(sent_rows, w_up, preferred_element_type=jnp.float32), 0.0
    ).astype(jnp.bfloat16)
    input_flattened = adapter_input_piece.reshape(
        language_count * adapter_rank, adapter_input_piece.shape[2]
    )
    reduced_rank = lax.dot_general(
        hidden_state, input_flattened, (((1,), (1,)), ((), ())), preferred_element_type=jnp.float32
    )
    column_position = jnp.arange(language_count * adapter_rank, dtype=jnp.int32) // adapter_rank
    keep_mask = slot_codes[:, None] - 1 == column_position[None, :]
    reduced_rank = jnp.where(keep_mask, reduced_rank, 0.0).astype(jnp.bfloat16)
    output_flattened = adapter_output_full.reshape(
        language_count * adapter_rank, adapter_output_full.shape[2]
    )
    adapter_update = jnp.dot(reduced_rank, output_flattened, preferred_element_type=jnp.float32)
    return jnp.dot(hidden_state, down_matrix, preferred_element_type=jnp.float32) + adapter_update


def build_send(tokens, expert_ids, language, lang_slot, expert_count, capacity):
    tok_count = tokens.shape[0]
    flat_route = jnp.concatenate([expert_ids[:, 0], expert_ids[:, 1]])
    expert_range = jnp.arange(expert_count, dtype=jnp.int32)
    one_hot = (flat_route[:, None] == expert_range[None, :]).astype(jnp.int32)
    before = jnp.cumsum(one_hot, axis=0) - one_hot
    position = jnp.sum(before * one_hot, axis=1)
    slot_of_row = flat_route * capacity + position
    slot_range = jnp.arange(expert_count * capacity, dtype=jnp.int32)
    row_range = jnp.arange(2 * tok_count, dtype=jnp.int32)
    source = jnp.sum(
        jnp.where(slot_of_row[None, :] == slot_range[:, None], row_range[None, :] + 1, 0), axis=1
    )
    filled = source > 0
    token_index = jnp.where(filled, source - 1, 0) % tok_count
    lang_range = jnp.arange(lang_slot.shape[0], dtype=jnp.int32)
    token_slot = jnp.sum(
        jnp.where(language[:, None] == lang_range[None, :], lang_slot[None, :], 0), axis=1
    )
    sent_rows = jnp.where(
        filled[:, None], jnp.take(tokens, token_index, axis=0), jnp.zeros((), tokens.dtype)
    )
    slot_codes = jnp.where(filled, jnp.take(token_slot, token_index) + 1, 0)
    return (
        sent_rows.reshape(expert_count, capacity, -1),
        slot_codes.reshape(expert_count, capacity),
        slot_of_row,
    )


def local(
    tokens,
    expert_ids,
    combine,
    language,
    lang_slot,
    up_weight,
    down_weight,
    adapter_in,
    adapter_out,
):
    tok_count = tokens.shape[0]
    model_width = tokens.shape[1]
    expert_count = lax.axis_size("expert")
    dp_count = lax.axis_size("dp")
    capacity = 3 * tok_count // expert_count
    send_rows, send_codes, slot_of_row = build_send(
        tokens, expert_ids, language, lang_slot, expert_count, capacity
    )
    got_rows, got_codes = (
        lax.all_to_all(send_rows, "expert", split_axis=0, concat_axis=0, tiled=True),
        lax.all_to_all(send_codes, "expert", split_axis=0, concat_axis=0, tiled=True),
    )
    in_part = lax.all_to_all(adapter_in, "dp", split_axis=3, concat_axis=0, tiled=True)
    all_rows, all_codes, out_full = (
        lax.all_gather(got_rows, "dp", axis=0, tiled=True),
        lax.all_gather(got_codes, "dp", axis=0, tiled=True),
        lax.all_gather(adapter_out, "dp", axis=0, tiled=True),
    )
    partial_term = expert_part(
        all_rows.reshape(-1, model_width),
        all_codes.reshape(-1),
        up_weight[0],
        down_weight[0],
        in_part[:, 0],
        out_full[:, 0],
    )
    rounded_term = partial_term.astype(jnp.bfloat16)
    summed = lax.psum_scatter(
        rounded_term.reshape(dp_count, expert_count, capacity, model_width),
        "dp",
        scatter_dimension=0,
        tiled=True,
    ).astype(jnp.float32)
    result_rows = summed.astype(jnp.bfloat16).reshape(expert_count, capacity, model_width)
    returned = lax.all_to_all(result_rows, "expert", split_axis=0, concat_axis=0, tiled=True)
    flat_back = returned.reshape(expert_count * capacity, model_width)
    picked = jnp.take(flat_back, slot_of_row, axis=0).astype(jnp.float32)
    mixed_out = combine[:, 0:1] * picked[:tok_count] + combine[:, 1:2] * picked[tok_count:]
    return mixed_out.astype(jnp.bfloat16)


def solution(mesh):
    placed = (
        P(("expert", "dp"), None),
        P(("expert", "dp"), None),
        P(("expert", "dp"), None),
        P(("expert", "dp")),
        P(),
        P("expert", None, "dp"),
        P("expert", "dp", None),
        P("dp", "expert", None, None),
        P("dp", "expert", None, None),
    )
    pairs = mesh.shape["dp"] == 4 and mesh.shape["expert"] == 8
    body = local_pairs if pairs else local
    return jax.shard_map(
        body, mesh=mesh, in_specs=placed, out_specs=P(("expert", "dp"), None), check_vma=False
    )
```

```python
import functools

import jax
import jax.numpy as jnp
from jax import lax
from jax.experimental import pallas as pl
from jax.experimental.pallas import tpu as pltpu
from jax.sharding import PartitionSpec as P

ORDER = tuple(
    "e6 e7 e1 a d:e7 y0:e6 u e4:d,e1 b:u y3:a,d e5 r0:e4 e3:b r3 y2:e5 e2:d y1:e2 o7 o6 r2:r3 r1:y2 o4 o5:o7 o2:r2 o1:y1 "
    "o3:r1".split()
)

F32 = jnp.float32
BF16 = jnp.bfloat16
VMEM = pl.BlockSpec(memory_space=pltpu.VMEM)
SMEM = pl.BlockSpec(memory_space=pltpu.SMEM)


def iota(shape, dim):
    return lax.broadcasted_iota(jnp.int32, shape, dim)


def row_places(hit):
    count = hit.shape[1]
    earlier = (iota((count, count), 0) < iota((count, count), 1)).astype(BF16)
    place = jnp.dot(hit.astype(F32).astype(BF16), earlier, preferred_element_type=F32)
    return jnp.where(hit, place, -1.0)


def prep_kernel(cap, slot_ref, ids_ref, lang_ref, tok_ref, in_ref, out_ref, mine, theirs, *outs):
    half = in_ref.shape[1] // 2
    y = lax.div(lax.axis_index("dp"), 2)
    for ref, at in ((mine, y), (theirs, 1 - y)):
        ref[:, :half] = in_ref[:, pl.ds(pl.multiple_of(at * half, half), half)]
        ref[:, half:] = out_ref[...]
    experts = len(outs)
    count, width = tok_ref.shape
    me = lax.axis_index("expert")
    first, second = ids_ref[0:1, :], ids_ref[1:2, :]
    expert = iota((experts, count), 0) ^ me
    place = row_places((first == expert) | (second == expert))
    want = iota((cap, count), 0).astype(F32)
    select = jnp.concatenate(
        [(place[j : j + 1, :] == want).astype(F32).astype(BF16) for j in range(experts)], axis=0
    )
    lang = lang_ref[...]
    slot = jnp.zeros_like(lang)
    for i in range(slot_ref.shape[0]):
        slot = jnp.where(lang == i, slot_ref[i] + 1, slot)
    code = jnp.broadcast_to(slot.astype(F32).astype(BF16), (128, count))
    rows = jnp.dot(select, tok_ref[...], preferred_element_type=F32).astype(BF16)
    codes = lax.dot_general(select, code, (((1,), (1,)), ((), ())), preferred_element_type=F32)
    codes = codes.astype(BF16)
    for j in range(experts):
        outs[j][:, :width] = rows[j * cap : (j + 1) * cap]
        outs[j][:, width:] = codes[j * cap : (j + 1) * cap]


def expert_kernel(
    rank, peer_ref, own_a_ref, own_b_ref, up_a, up_b, down_a, down_b, ain_ref, aout_ref, send_ref,
    keep_ref, rows_buf, hid_buf,
):
    width, hid = up_a.shape
    columns = aout_ref.shape[0]
    half = peer_ref.shape[0]
    dp = lax.axis_index("dp")
    column = iota((1, columns), 1)
    part = lax.div(column, columns // 4)
    owner = dp ^ (lax.rem(part, 2) * 2 + lax.div(part, 2))
    each = columns // 4 // rank
    slot = owner * each + lax.rem(lax.div(column, rank), each) + 1
    slot = slot.astype(F32)
    at = 0
    codes = []
    for ref in (peer_ref, own_a_ref, own_b_ref):
        rows_buf[at : at + ref.shape[0], :] = ref[:, :width]
        codes.append(ref[:, width:].astype(F32))
        at += ref.shape[0]
    keep = jnp.concatenate(codes, axis=0) == slot
    rows = rows_buf[...]
    step = 512
    low = []
    core = lax.rem(dp, 2)
    for h, up in enumerate((up_a, up_b)):
        for b in range(hid // step):
            hidden = jnp.dot(rows, up[:, b * step : (b + 1) * step], preferred_element_type=F32)
            hid_buf[h, :, b * step : (b + 1) * step] = jnp.maximum(hidden, 0.0).astype(BF16)
        where = pl.ds(pl.multiple_of((core ^ h) * hid, hid), hid)
        one = lax.dot_general(
            hid_buf[h], ain_ref[:, where], (((1,), (1,)), ((), ())), preferred_element_type=F32
        )
        low.append(jnp.where(keep, one, 0.0).astype(BF16).astype(F32))
    low = (low[0] + low[1]).astype(BF16)
    for b in range(width // step):
        span = slice(b * step, (b + 1) * step)
        total = jnp.dot(hid_buf[0], down_a[:, span], preferred_element_type=F32)
        total += jnp.dot(hid_buf[1], down_b[:, span], preferred_element_type=F32)
        total += jnp.dot(low, aout_ref[:, span], preferred_element_type=F32)
        send_ref[:, span] = total[:half].astype(BF16)
        keep_ref[:, span] = total[half:]


def mix_kernel(cap, ids_ref, combine_ref, *refs):
    backs, out_ref = refs[:-1], refs[-1]
    experts = len(backs)
    count = ids_ref.shape[0]
    me = lax.axis_index("expert")
    first, second = ids_ref[:, 0:1] ^ me, ids_ref[:, 1:2] ^ me
    lane = iota((count, 128), 1)
    hit = ((first == lane) | (second == lane)).astype(F32).astype(BF16)
    earlier = (iota((count, count), 1) < iota((count, count), 0)).astype(F32).astype(BF16)
    place = jnp.dot(earlier, hit, preferred_element_type=F32)
    back = jnp.concatenate([b[...] for b in backs], axis=0)
    spot = iota((count, experts * cap), 1).astype(F32)
    mixed = None
    for k, choice in enumerate((first, second)):
        at = jnp.sum(jnp.where(choice == lane, place, 0.0), axis=1, keepdims=True)
        at = at + (choice * cap).astype(F32)
        select = (at == spot).astype(F32).astype(BF16)
        picked = jnp.dot(select, back, preferred_element_type=F32)
        term = combine_ref[:, k : k + 1] * picked
        mixed = term if mixed is None else mixed + term
    out_ref[...] = mixed.astype(BF16)


def after(x, *done):
    return lax.optimization_barrier((x,) + done)[0]


def flip(x, axis, bit):
    size = lax.axis_size(axis)
    return lax.ppermute(x, axis, [(i, i ^ bit) for i in range(size)])


def local_pairs(
    tokens, expert_ids, combine, language, lang_slot, up_weight, down_weight, adapter_in, adapter_out
):
    count, width = tokens.shape
    experts = lax.axis_size("expert")
    cap = 3 * count // experts
    slots, _, rank, hid_all = adapter_in.shape
    up, down = up_weight[0], down_weight[0]
    hid = up.shape[1]

    flat_in = adapter_in.reshape(slots * rank, hid_all)
    flat_out = adapter_out.reshape(slots * rank, width)
    prep = pl.pallas_call(
        functools.partial(prep_kernel, cap),
        out_shape=[jax.ShapeDtypeStruct((slots * rank, 2 * hid + width), BF16)] * 2
        + [jax.ShapeDtypeStruct((cap, width + 128), BF16)] * experts,
        in_specs=[SMEM] + [VMEM] * 5,
        out_specs=[VMEM] * (2 + experts),
        cost_estimate=pl.CostEstimate(flops=10**8, bytes_accessed=2 * 10**6, transcendentals=0),
        name="prep",
    )(lang_slot, expert_ids.T, language[None, :], tokens, flat_in, flat_out)
    mine, theirs, send = prep[0], prep[1], prep[2:]

    def run_expert(peer, a, b):
        full = state["full"]
        return pl.pallas_call(
            functools.partial(expert_kernel, rank),
            out_shape=[
                jax.ShapeDtypeStruct((2 * cap, width), BF16),
                jax.ShapeDtypeStruct((2 * cap, width), F32),
            ],
            in_specs=[VMEM] * 9,
            out_specs=[VMEM, VMEM],
            scratch_shapes=[
                pltpu.VMEM((4 * cap, width), BF16),
                pltpu.VMEM((2, 4 * cap, hid), BF16),
            ],
            compiler_params=pltpu.CompilerParams(vmem_limit_bytes=24 * 2**20),
            cost_estimate=pl.CostEstimate(
                flops=32 * cap * width * hid, bytes_accessed=10 * 2**20, transcendentals=0
            ),
            name="expert",
        )(peer, a, b, up, got["u"], down, got["d"], full[:, : 2 * hid], full[:, 2 * hid :])

    def both(a, b):
        return jnp.concatenate([a, b], axis=0)

    def join(own, back):
        done = (own + back.astype(F32)).astype(BF16)
        return done[:cap], done[cap:]

    got, parts, sums, state = {"e0": send[0]}, {}, {}, {}

    def rows_of(k):
        return got["e%d" % (2 * k)], got["e%d" % (2 * k + 1)]

    def run_chunk(k):
        if k not in parts:
            if "full" not in state:
                state["full"] = both(state["pair"], got["b"])
            peer = got["y%d" % k]
            if "last" in state:
                peer = after(peer, state["last"])
            parts[k] = run_expert(peer, *rows_of(k))
            state["last"] = parts[k][0]
        return parts[k]

    def run_sum(k):
        if k not in sums:
            sums[k] = join(run_chunk(k)[1], got["r%d" % k])
        return sums[k]

    def source(name):
        kind, number = name[0], int(name[1:] or 0)
        if kind == "e":
            return send[number], "expert", number
        if kind == "y":
            return both(*rows_of(number)), "dp", 2
        if kind == "r":
            return run_chunk(number)[0], "dp", 2
        if kind == "o":
            return run_sum(number // 2)[number % 2], "expert", number
        if kind == "a":
            return theirs, "dp", 2
        if kind == "b":
            state["pair"] = both(mine, got["a"])
            return state["pair"], "dp", 1
        return (up if kind == "u" else down), "dp", 1

    for item in ORDER:
        name, _, gates = item.partition(":")
        x, axis, bit = source(name)
        if gates:
            x = after(x, *[got[g] for g in gates.split(",")])
        got[name] = flip(x, axis, bit)
    backs = [run_sum(0)[0]] + [got["o%d" % j] for j in range(1, experts)]

    return pl.pallas_call(
        functools.partial(mix_kernel, cap),
        out_shape=jax.ShapeDtypeStruct((count, width), BF16),
        in_specs=[VMEM] * (2 + experts),
        out_specs=VMEM,
        compiler_params=pltpu.CompilerParams(vmem_limit_bytes=8 * 2**20),
        cost_estimate=pl.CostEstimate(flops=2 * 10**8, bytes_accessed=2 * 10**6, transcendentals=0),
        name="mix",
    )(expert_ids, combine, *backs)


def expert_part(sent_rows, slot_codes, w_up, down_matrix, adapter_input_piece, adapter_output_full):
    language_count = adapter_input_piece.shape[0]
    adapter_rank = adapter_input_piece.shape[1]
    hidden_state = jnp.maximum(
        jnp.dot(sent_rows, w_up, preferred_element_type=jnp.float32), 0.0
    ).astype(jnp.bfloat16)
    input_flattened = adapter_input_piece.reshape(
        language_count * adapter_rank, adapter_input_piece.shape[2]
    )
    reduced_rank = lax.dot_general(
        hidden_state, input_flattened, (((1,), (1,)), ((), ())), preferred_element_type=jnp.float32
    )
    column_position = jnp.arange(language_count * adapter_rank, dtype=jnp.int32) // adapter_rank
    keep_mask = slot_codes[:, None] - 1 == column_position[None, :]
    reduced_rank = jnp.where(keep_mask, reduced_rank, 0.0).astype(jnp.bfloat16)
    output_flattened = adapter_output_full.reshape(
        language_count * adapter_rank, adapter_output_full.shape[2]
    )
    adapter_update = jnp.dot(reduced_rank, output_flattened, preferred_element_type=jnp.float32)
    return jnp.dot(hidden_state, down_matrix, preferred_element_type=jnp.float32) + adapter_update


def build_send(tokens, expert_ids, language, lang_slot, expert_count, capacity):
    tok_count = tokens.shape[0]
    flat_route = jnp.concatenate([expert_ids[:, 0], expert_ids[:, 1]])
    expert_range = jnp.arange(expert_count, dtype=jnp.int32)
    one_hot = (flat_route[:, None] == expert_range[None, :]).astype(jnp.int32)
    before = jnp.cumsum(one_hot, axis=0) - one_hot
    position = jnp.sum(before * one_hot, axis=1)
    slot_of_row = flat_route * capacity + position
    slot_range = jnp.arange(expert_count * capacity, dtype=jnp.int32)
    row_range = jnp.arange(2 * tok_count, dtype=jnp.int32)
    source = jnp.sum(
        jnp.where(slot_of_row[None, :] == slot_range[:, None], row_range[None, :] + 1, 0), axis=1
    )
    filled = source > 0
    token_index = jnp.where(filled, source - 1, 0) % tok_count
    lang_range = jnp.arange(lang_slot.shape[0], dtype=jnp.int32)
    token_slot = jnp.sum(
        jnp.where(language[:, None] == lang_range[None, :], lang_slot[None, :], 0), axis=1
    )
    sent_rows = jnp.where(
        filled[:, None], jnp.take(tokens, token_index, axis=0), jnp.zeros((), tokens.dtype)
    )
    slot_codes = jnp.where(filled, jnp.take(token_slot, token_index) + 1, 0)
    return (
        sent_rows.reshape(expert_count, capacity, -1),
        slot_codes.reshape(expert_count, capacity),
        slot_of_row,
    )


def local(
    tokens,
    expert_ids,
    combine,
    language,
    lang_slot,
    up_weight,
    down_weight,
    adapter_in,
    adapter_out,
):
    tok_count = tokens.shape[0]
    model_width = tokens.shape[1]
    expert_count = lax.axis_size("expert")
    dp_count = lax.axis_size("dp")
    capacity = 3 * tok_count // expert_count
    send_rows, send_codes, slot_of_row = build_send(
        tokens, expert_ids, language, lang_slot, expert_count, capacity
    )
    got_rows, got_codes = (
        lax.all_to_all(send_rows, "expert", split_axis=0, concat_axis=0, tiled=True),
        lax.all_to_all(send_codes, "expert", split_axis=0, concat_axis=0, tiled=True),
    )
    in_part = lax.all_to_all(adapter_in, "dp", split_axis=3, concat_axis=0, tiled=True)
    all_rows, all_codes, out_full = (
        lax.all_gather(got_rows, "dp", axis=0, tiled=True),
        lax.all_gather(got_codes, "dp", axis=0, tiled=True),
        lax.all_gather(adapter_out, "dp", axis=0, tiled=True),
    )
    partial_term = expert_part(
        all_rows.reshape(-1, model_width),
        all_codes.reshape(-1),
        up_weight[0],
        down_weight[0],
        in_part[:, 0],
        out_full[:, 0],
    )
    rounded_term = partial_term.astype(jnp.bfloat16)
    summed = lax.psum_scatter(
        rounded_term.reshape(dp_count, expert_count, capacity, model_width),
        "dp",
        scatter_dimension=0,
        tiled=True,
    ).astype(jnp.float32)
    result_rows = summed.astype(jnp.bfloat16).reshape(expert_count, capacity, model_width)
    returned = lax.all_to_all(result_rows, "expert", split_axis=0, concat_axis=0, tiled=True)
    flat_back = returned.reshape(expert_count * capacity, model_width)
    picked = jnp.take(flat_back, slot_of_row, axis=0).astype(jnp.float32)
    mixed_out = combine[:, 0:1] * picked[:tok_count] + combine[:, 1:2] * picked[tok_count:]
    return mixed_out.astype(jnp.bfloat16)


def solution(mesh):
    placed = (
        P(("expert", "dp"), None),
        P(("expert", "dp"), None),
        P(("expert", "dp"), None),
        P(("expert", "dp")),
        P(),
        P("expert", None, "dp"),
        P("expert", "dp", None),
        P("dp", "expert", None, None),
        P("dp", "expert", None, None),
    )
    pairs = mesh.shape["dp"] == 4 and mesh.shape["expert"] == 8
    body = local_pairs if pairs else local
    return jax.shard_map(
        body, mesh=mesh, in_specs=placed, out_specs=P(("expert", "dp"), None), check_vma=False
    )
```

```python
import functools

import jax
import jax.numpy as jnp
from jax import lax
from jax.experimental import pallas as pl
from jax.experimental.pallas import tpu as pltpu
from jax.sharding import PartitionSpec as P

ORDER = (
    "e6", "e7", "e1", "a", "d:e7", "y0:e6", "u", "e4:d,e1", "b:u", "y3:a,d", "e5", "r0", "e3:b",
    "r3", "y2:e5", "e2:d", "y1:e2", "o7", "o6", "r2:r3", "r1:E0,y2", "o4", "o5:o7", "o2:r2",
    "o1:y1", "o3:r1",
)

F32 = jnp.float32
BF16 = jnp.bfloat16
VMEM = pl.BlockSpec(memory_space=pltpu.VMEM)
SMEM = pl.BlockSpec(memory_space=pltpu.SMEM)


def iota(shape, dim):
    return lax.broadcasted_iota(jnp.int32, shape, dim)


def row_places(hit):
    count = hit.shape[1]
    earlier = (iota((count, count), 0) < iota((count, count), 1)).astype(BF16)
    place = jnp.dot(hit.astype(F32).astype(BF16), earlier, preferred_element_type=F32)
    return jnp.where(hit, place, -1.0)


def prep_kernel(cap, slot_ref, ids_ref, lang_ref, tok_ref, in_ref, out_ref, mine, theirs, *outs):
    half = in_ref.shape[1] // 2
    y = lax.div(lax.axis_index("dp"), 2)
    for ref, at in ((mine, y), (theirs, 1 - y)):
        ref[:, :half] = in_ref[:, pl.ds(pl.multiple_of(at * half, half), half)]
        ref[:, half:] = out_ref[...]
    experts = len(outs)
    count, width = tok_ref.shape
    me = lax.axis_index("expert")
    first, second = ids_ref[0:1, :], ids_ref[1:2, :]
    expert = iota((experts, count), 0) ^ me
    place = row_places((first == expert) | (second == expert))
    want = iota((cap, count), 0).astype(F32)
    select = jnp.concatenate(
        [(place[j : j + 1, :] == want).astype(F32).astype(BF16) for j in range(experts)], axis=0
    )
    lang = lang_ref[...]
    slot = jnp.zeros_like(lang)
    for i in range(slot_ref.shape[0]):
        slot = jnp.where(lang == i, slot_ref[i] + 1, slot)
    code = jnp.broadcast_to(slot.astype(F32).astype(BF16), (128, count))
    rows = jnp.dot(select, tok_ref[...], preferred_element_type=F32).astype(BF16)
    codes = lax.dot_general(select, code, (((1,), (1,)), ((), ())), preferred_element_type=F32)
    codes = codes.astype(BF16)
    for j in range(experts):
        outs[j][:, :width] = rows[j * cap : (j + 1) * cap]
        outs[j][:, width:] = codes[j * cap : (j + 1) * cap]


def expert_kernel(
    rank, peer_ref, own_a_ref, own_b_ref, up_a, up_b, down_a, down_b, ain_ref, aout_ref, send_ref,
    keep_ref, rows_buf, hid_buf,
):
    width, hid = up_a.shape
    columns = aout_ref.shape[0]
    half = peer_ref.shape[0]
    dp = lax.axis_index("dp")
    column = iota((1, columns), 1)
    part = lax.div(column, columns // 4)
    owner = dp ^ (lax.rem(part, 2) * 2 + lax.div(part, 2))
    each = columns // 4 // rank
    slot = owner * each + lax.rem(lax.div(column, rank), each) + 1
    slot = slot.astype(F32)
    at = 0
    codes = []
    for ref in (peer_ref, own_a_ref, own_b_ref):
        rows_buf[at : at + ref.shape[0], :] = ref[:, :width]
        codes.append(ref[:, width:].astype(F32))
        at += ref.shape[0]
    keep = jnp.concatenate(codes, axis=0) == slot
    rows = rows_buf[...]
    step = 512
    low = []
    core = lax.rem(dp, 2)
    for h, up in enumerate((up_a, up_b)):
        for b in range(hid // step):
            hidden = jnp.dot(rows, up[:, b * step : (b + 1) * step], preferred_element_type=F32)
            hid_buf[h, :, b * step : (b + 1) * step] = jnp.maximum(hidden, 0.0).astype(BF16)
        where = pl.ds(pl.multiple_of((core ^ h) * hid, hid), hid)
        one = lax.dot_general(
            hid_buf[h], ain_ref[:, where], (((1,), (1,)), ((), ())), preferred_element_type=F32
        )
        low.append(jnp.where(keep, one, 0.0).astype(BF16).astype(F32))
    low = (low[0] + low[1]).astype(BF16)
    for b in range(width // step):
        span = slice(b * step, (b + 1) * step)
        total = jnp.dot(hid_buf[0], down_a[:, span], preferred_element_type=F32)
        total += jnp.dot(hid_buf[1], down_b[:, span], preferred_element_type=F32)
        total += jnp.dot(low, aout_ref[:, span], preferred_element_type=F32)
        send_ref[:, span] = total[:half].astype(BF16)
        keep_ref[:, span] = total[half:]


def mix_kernel(cap, ids_ref, combine_ref, *refs):
    backs, out_ref = refs[:-1], refs[-1]
    experts = len(backs)
    count = ids_ref.shape[0]
    me = lax.axis_index("expert")
    first, second = ids_ref[:, 0:1] ^ me, ids_ref[:, 1:2] ^ me
    lane = iota((count, 128), 1)
    hit = ((first == lane) | (second == lane)).astype(F32).astype(BF16)
    earlier = (iota((count, count), 1) < iota((count, count), 0)).astype(F32).astype(BF16)
    place = jnp.dot(earlier, hit, preferred_element_type=F32)
    back = jnp.concatenate([b[...] for b in backs], axis=0)
    spot = iota((count, experts * cap), 1).astype(F32)
    mixed = None
    for k, choice in enumerate((first, second)):
        at = jnp.sum(jnp.where(choice == lane, place, 0.0), axis=1, keepdims=True)
        at = at + (choice * cap).astype(F32)
        select = (at == spot).astype(F32).astype(BF16)
        picked = jnp.dot(select, back, preferred_element_type=F32)
        term = combine_ref[:, k : k + 1] * picked
        mixed = term if mixed is None else mixed + term
    out_ref[...] = mixed.astype(BF16)


def after(x, *done):
    return lax.optimization_barrier((x,) + done)[0]


def flip(x, axis, bit):
    size = lax.axis_size(axis)
    return lax.ppermute(x, axis, [(i, i ^ bit) for i in range(size)])


def local_pairs(
    tokens, expert_ids, combine, language, lang_slot, up_weight, down_weight, adapter_in, adapter_out
):
    count, width = tokens.shape
    experts = lax.axis_size("expert")
    cap = 3 * count // experts
    slots, _, rank, hid_all = adapter_in.shape
    up, down = up_weight[0], down_weight[0]
    hid = up.shape[1]

    flat_in = adapter_in.reshape(slots * rank, hid_all)
    flat_out = adapter_out.reshape(slots * rank, width)
    prep = pl.pallas_call(
        functools.partial(prep_kernel, cap),
        out_shape=[jax.ShapeDtypeStruct((slots * rank, 2 * hid + width), BF16)] * 2
        + [jax.ShapeDtypeStruct((cap, width + 128), BF16)] * experts,
        in_specs=[SMEM] + [VMEM] * 5,
        out_specs=[VMEM] * (2 + experts),
        cost_estimate=pl.CostEstimate(flops=10**8, bytes_accessed=2 * 10**6, transcendentals=0),
        name="prep",
    )(lang_slot, expert_ids.T, language[None, :], tokens, flat_in, flat_out)
    mine, theirs, send = prep[0], prep[1], prep[2:]

    def run_expert(peer, a, b):
        full = state["full"]
        return pl.pallas_call(
            functools.partial(expert_kernel, rank),
            out_shape=[
                jax.ShapeDtypeStruct((2 * cap, width), BF16),
                jax.ShapeDtypeStruct((2 * cap, width), F32),
            ],
            in_specs=[VMEM] * 9,
            out_specs=[VMEM, VMEM],
            scratch_shapes=[
                pltpu.VMEM((4 * cap, width), BF16),
                pltpu.VMEM((2, 4 * cap, hid), BF16),
            ],
            compiler_params=pltpu.CompilerParams(vmem_limit_bytes=24 * 2**20),
            cost_estimate=pl.CostEstimate(
                flops=32 * cap * width * hid, bytes_accessed=10 * 2**20, transcendentals=0
            ),
            name="expert",
        )(peer, a, b, up, got["u"], down, got["d"], full[:, : 2 * hid], full[:, 2 * hid :])

    def both(a, b):
        return jnp.concatenate([a, b], axis=0)

    def join(own, back):
        done = (own + back.astype(F32)).astype(BF16)
        return done[:cap], done[cap:]

    got, parts, sums, state = {"e0": send[0]}, {}, {}, {}

    def rows_of(k):
        return got["e%d" % (2 * k)], got["e%d" % (2 * k + 1)]

    def run_chunk(k):
        if k not in parts:
            if "full" not in state:
                state["full"] = both(state["pair"], got["b"])
            peer = got["y%d" % k]
            if "last" in state:
                peer = after(peer, state["last"])
            parts[k] = run_expert(peer, *rows_of(k))
            state["last"] = got["E%d" % k] = parts[k][0]
        return parts[k]

    def run_sum(k):
        if k not in sums:
            sums[k] = join(run_chunk(k)[1], got["r%d" % k])
        return sums[k]

    def source(name):
        kind, number = name[0], int(name[1:] or 0)
        if kind == "e":
            return send[number], "expert", number
        if kind == "y":
            return both(*rows_of(number)), "dp", 2
        if kind == "r":
            return run_chunk(number)[0], "dp", 2
        if kind == "o":
            return run_sum(number // 2)[number % 2], "expert", number
        if kind == "a":
            return theirs, "dp", 2
        if kind == "b":
            state["pair"] = both(mine, got["a"])
            return state["pair"], "dp", 1
        return (up if kind == "u" else down), "dp", 1

    for item in ORDER:
        name, _, gates = item.partition(":")
        x, axis, bit = source(name)
        if gates:
            x = after(x, *[got[g] for g in gates.split(",")])
        got[name] = flip(x, axis, bit)
    backs = [run_sum(0)[0]] + [got["o%d" % j] for j in range(1, experts)]

    return pl.pallas_call(
        functools.partial(mix_kernel, cap),
        out_shape=jax.ShapeDtypeStruct((count, width), BF16),
        in_specs=[VMEM] * (2 + experts),
        out_specs=VMEM,
        compiler_params=pltpu.CompilerParams(vmem_limit_bytes=8 * 2**20),
        cost_estimate=pl.CostEstimate(flops=2 * 10**8, bytes_accessed=2 * 10**6, transcendentals=0),
        name="mix",
    )(expert_ids, combine, *backs)


def expert_part(sent_rows, slot_codes, w_up, down_matrix, adapter_input_piece, adapter_output_full):
    language_count = adapter_input_piece.shape[0]
    adapter_rank = adapter_input_piece.shape[1]
    hidden_state = jnp.maximum(
        jnp.dot(sent_rows, w_up, preferred_element_type=jnp.float32), 0.0
    ).astype(jnp.bfloat16)
    input_flattened = adapter_input_piece.reshape(
        language_count * adapter_rank, adapter_input_piece.shape[2]
    )
    reduced_rank = lax.dot_general(
        hidden_state, input_flattened, (((1,), (1,)), ((), ())), preferred_element_type=jnp.float32
    )
    column_position = jnp.arange(language_count * adapter_rank, dtype=jnp.int32) // adapter_rank
    keep_mask = slot_codes[:, None] - 1 == column_position[None, :]
    reduced_rank = jnp.where(keep_mask, reduced_rank, 0.0).astype(jnp.bfloat16)
    output_flattened = adapter_output_full.reshape(
        language_count * adapter_rank, adapter_output_full.shape[2]
    )
    adapter_update = jnp.dot(reduced_rank, output_flattened, preferred_element_type=jnp.float32)
    return jnp.dot(hidden_state, down_matrix, preferred_element_type=jnp.float32) + adapter_update


def build_send(tokens, expert_ids, language, lang_slot, expert_count, capacity):
    tok_count = tokens.shape[0]
    flat_route = jnp.concatenate([expert_ids[:, 0], expert_ids[:, 1]])
    expert_range = jnp.arange(expert_count, dtype=jnp.int32)
    one_hot = (flat_route[:, None] == expert_range[None, :]).astype(jnp.int32)
    before = jnp.cumsum(one_hot, axis=0) - one_hot
    position = jnp.sum(before * one_hot, axis=1)
    slot_of_row = flat_route * capacity + position
    slot_range = jnp.arange(expert_count * capacity, dtype=jnp.int32)
    row_range = jnp.arange(2 * tok_count, dtype=jnp.int32)
    source = jnp.sum(
        jnp.where(slot_of_row[None, :] == slot_range[:, None], row_range[None, :] + 1, 0), axis=1
    )
    filled = source > 0
    token_index = jnp.where(filled, source - 1, 0) % tok_count
    lang_range = jnp.arange(lang_slot.shape[0], dtype=jnp.int32)
    token_slot = jnp.sum(
        jnp.where(language[:, None] == lang_range[None, :], lang_slot[None, :], 0), axis=1
    )
    sent_rows = jnp.where(
        filled[:, None], jnp.take(tokens, token_index, axis=0), jnp.zeros((), tokens.dtype)
    )
    slot_codes = jnp.where(filled, jnp.take(token_slot, token_index) + 1, 0)
    return (
        sent_rows.reshape(expert_count, capacity, -1),
        slot_codes.reshape(expert_count, capacity),
        slot_of_row,
    )


def local(
    tokens,
    expert_ids,
    combine,
    language,
    lang_slot,
    up_weight,
    down_weight,
    adapter_in,
    adapter_out,
):
    tok_count = tokens.shape[0]
    model_width = tokens.shape[1]
    expert_count = lax.axis_size("expert")
    dp_count = lax.axis_size("dp")
    capacity = 3 * tok_count // expert_count
    send_rows, send_codes, slot_of_row = build_send(
        tokens, expert_ids, language, lang_slot, expert_count, capacity
    )
    got_rows, got_codes = (
        lax.all_to_all(send_rows, "expert", split_axis=0, concat_axis=0, tiled=True),
        lax.all_to_all(send_codes, "expert", split_axis=0, concat_axis=0, tiled=True),
    )
    in_part = lax.all_to_all(adapter_in, "dp", split_axis=3, concat_axis=0, tiled=True)
    all_rows, all_codes, out_full = (
        lax.all_gather(got_rows, "dp", axis=0, tiled=True),
        lax.all_gather(got_codes, "dp", axis=0, tiled=True),
        lax.all_gather(adapter_out, "dp", axis=0, tiled=True),
    )
    partial_term = expert_part(
        all_rows.reshape(-1, model_width),
        all_codes.reshape(-1),
        up_weight[0],
        down_weight[0],
        in_part[:, 0],
        out_full[:, 0],
    )
    rounded_term = partial_term.astype(jnp.bfloat16)
    summed = lax.psum_scatter(
        rounded_term.reshape(dp_count, expert_count, capacity, model_width),
        "dp",
        scatter_dimension=0,
        tiled=True,
    ).astype(jnp.float32)
    result_rows = summed.astype(jnp.bfloat16).reshape(expert_count, capacity, model_width)
    returned = lax.all_to_all(result_rows, "expert", split_axis=0, concat_axis=0, tiled=True)
    flat_back = returned.reshape(expert_count * capacity, model_width)
    picked = jnp.take(flat_back, slot_of_row, axis=0).astype(jnp.float32)
    mixed_out = combine[:, 0:1] * picked[:tok_count] + combine[:, 1:2] * picked[tok_count:]
    return mixed_out.astype(jnp.bfloat16)


def solution(mesh):
    placed = (
        P(("expert", "dp"), None),
        P(("expert", "dp"), None),
        P(("expert", "dp"), None),
        P(("expert", "dp")),
        P(),
        P("expert", None, "dp"),
        P("expert", "dp", None),
        P("dp", "expert", None, None),
        P("dp", "expert", None, None),
    )
    pairs = mesh.shape["dp"] == 4 and mesh.shape["expert"] == 8
    body = local_pairs if pairs else local
    return jax.shard_map(
        body, mesh=mesh, in_specs=placed, out_specs=P(("expert", "dp"), None), check_vma=False
    )
```

```python
import functools

import jax
import jax.numpy as jnp
from jax import lax
from jax.experimental import pallas as pl
from jax.experimental.pallas import tpu as pltpu
from jax.sharding import PartitionSpec as P

ORDER = (
    "e6", "e7", "e1", "a", "d:e7", "y0:e6", "u", "e4:d,e1", "b:u", "y3:a,d", "e5", "r0", "e3:b",
    "r3", "y2:e5", "e2:d", "y1:e2", "o7", "o6", "r2:r3", "r1:E0,y2", "o4", "o5:o7", "o2:r2",
    "o1:y1", "o3:r1",
)

F32 = jnp.float32
BF16 = jnp.bfloat16
VMEM = pl.BlockSpec(memory_space=pltpu.VMEM)
SMEM = pl.BlockSpec(memory_space=pltpu.SMEM)


def iota(shape, dim):
    return lax.broadcasted_iota(jnp.int32, shape, dim)


def row_places(hit):
    count = hit.shape[1]
    earlier = (iota((count, count), 0) < iota((count, count), 1)).astype(BF16)
    place = jnp.dot(hit.astype(F32).astype(BF16), earlier, preferred_element_type=F32)
    return jnp.where(hit, place, -1.0)


def prep_kernel(cap, slot_ref, ids_ref, lang_ref, tok_ref, in_ref, out_ref, mine, theirs, *outs):
    half = in_ref.shape[1] // 2
    y = lax.div(lax.axis_index("dp"), 2)
    for ref, at in ((mine, y), (theirs, 1 - y)):
        ref[:, :half] = in_ref[:, pl.ds(pl.multiple_of(at * half, half), half)]
        ref[:, half:] = out_ref[...]
    experts = len(outs)
    count, width = tok_ref.shape
    me = lax.axis_index("expert")
    first, second = ids_ref[0:1, :], ids_ref[1:2, :]
    expert = iota((experts, count), 0) ^ me
    place = row_places((first == expert) | (second == expert))
    want = iota((cap, count), 0).astype(F32)
    select = jnp.concatenate(
        [(place[j : j + 1, :] == want).astype(F32).astype(BF16) for j in range(experts)], axis=0
    )
    lang = lang_ref[...]
    slot = jnp.zeros_like(lang)
    for i in range(slot_ref.shape[0]):
        slot = jnp.where(lang == i, slot_ref[i] + 1, slot)
    code = jnp.broadcast_to(slot.astype(F32).astype(BF16), (128, count))
    rows = jnp.dot(select, tok_ref[...], preferred_element_type=F32).astype(BF16)
    codes = lax.dot_general(select, code, (((1,), (1,)), ((), ())), preferred_element_type=F32)
    codes = codes.astype(BF16)
    for j in range(experts):
        outs[j][:, :width] = rows[j * cap : (j + 1) * cap]
        outs[j][:, width:] = codes[j * cap : (j + 1) * cap]


def expert_kernel(
    rank, peer_ref, own_a_ref, own_b_ref, up_a, up_b, down_a, down_b, ain_ref, aout_ref, send_ref,
    keep_ref, rows_buf, hid_buf,
):
    width, hid = up_a.shape
    columns = aout_ref.shape[0]
    half = peer_ref.shape[0]
    dp = lax.axis_index("dp")
    column = iota((1, columns), 1)
    part = lax.div(column, columns // 4)
    owner = dp ^ (lax.rem(part, 2) * 2 + lax.div(part, 2))
    each = columns // 4 // rank
    slot = owner * each + lax.rem(lax.div(column, rank), each) + 1
    slot = slot.astype(F32)
    at = 0
    codes = []
    for ref in (peer_ref, own_a_ref, own_b_ref):
        rows_buf[at : at + ref.shape[0], :] = ref[:, :width]
        codes.append(ref[:, width:].astype(F32))
        at += ref.shape[0]
    keep = jnp.concatenate(codes, axis=0) == slot
    rows = rows_buf[...]
    step = 512
    low = []
    core = lax.rem(dp, 2)
    for h, up in enumerate((up_a, up_b)):
        for b in range(hid // step):
            hidden = jnp.dot(rows, up[:, b * step : (b + 1) * step], preferred_element_type=F32)
            hid_buf[h, :, b * step : (b + 1) * step] = jnp.maximum(hidden, 0.0).astype(BF16)
        where = pl.ds(pl.multiple_of((core ^ h) * hid, hid), hid)
        one = lax.dot_general(
            hid_buf[h], ain_ref[:, where], (((1,), (1,)), ((), ())), preferred_element_type=F32
        )
        low.append(jnp.where(keep, one, 0.0).astype(BF16).astype(F32))
    low = (low[0] + low[1]).astype(BF16)
    for b in range(width // step):
        span = slice(b * step, (b + 1) * step)
        total = jnp.dot(hid_buf[0], down_a[:, span], preferred_element_type=F32)
        total += jnp.dot(hid_buf[1], down_b[:, span], preferred_element_type=F32)
        total += jnp.dot(low, aout_ref[:, span], preferred_element_type=F32)
        send_ref[:, span] = total[:half].astype(BF16)
        keep_ref[:, span] = total[half:]


def mix_kernel(cap, ids_ref, combine_ref, *refs):
    backs, out_ref = refs[:-1], refs[-1]
    experts = len(backs)
    count = ids_ref.shape[0]
    me = lax.axis_index("expert")
    first, second = ids_ref[:, 0:1] ^ me, ids_ref[:, 1:2] ^ me
    lane = iota((count, 128), 1)
    hit = ((first == lane) | (second == lane)).astype(F32).astype(BF16)
    earlier = (iota((count, count), 1) < iota((count, count), 0)).astype(F32).astype(BF16)
    place = jnp.dot(earlier, hit, preferred_element_type=F32)
    back = jnp.concatenate([b[...] for b in backs], axis=0)
    spot = iota((count, experts * cap), 1).astype(F32)
    selects = []
    for choice in (first, second):
        at = jnp.sum(jnp.where(choice == lane, place, 0.0), axis=1, keepdims=True)
        at = at + (choice * cap).astype(F32)
        selects.append((at == spot).astype(F32).astype(BF16))
    picked = jnp.dot(jnp.concatenate(selects, axis=0), back, preferred_element_type=F32)
    mixed = combine_ref[:, 0:1] * picked[:count] + combine_ref[:, 1:2] * picked[count:]
    out_ref[...] = mixed.astype(BF16)


def after(x, *done):
    return lax.optimization_barrier((x,) + done)[0]


def flip(x, axis, bit):
    size = lax.axis_size(axis)
    return lax.ppermute(x, axis, [(i, i ^ bit) for i in range(size)])


def local_pairs(
    tokens, expert_ids, combine, language, lang_slot, up_weight, down_weight, adapter_in, adapter_out
):
    count, width = tokens.shape
    experts = lax.axis_size("expert")
    cap = 3 * count // experts
    slots, _, rank, hid_all = adapter_in.shape
    up, down = up_weight[0], down_weight[0]
    hid = up.shape[1]

    flat_in = adapter_in.reshape(slots * rank, hid_all)
    flat_out = adapter_out.reshape(slots * rank, width)
    prep = pl.pallas_call(
        functools.partial(prep_kernel, cap),
        out_shape=[jax.ShapeDtypeStruct((slots * rank, 2 * hid + width), BF16)] * 2
        + [jax.ShapeDtypeStruct((cap, width + 128), BF16)] * experts,
        in_specs=[SMEM] + [VMEM] * 5,
        out_specs=[VMEM] * (2 + experts),
        cost_estimate=pl.CostEstimate(flops=10**8, bytes_accessed=2 * 10**6, transcendentals=0),
        name="prep",
    )(lang_slot, expert_ids.T, language[None, :], tokens, flat_in, flat_out)
    mine, theirs, send = prep[0], prep[1], prep[2:]

    def run_expert(peer, a, b):
        full = state["full"]
        return pl.pallas_call(
            functools.partial(expert_kernel, rank),
            out_shape=[
                jax.ShapeDtypeStruct((2 * cap, width), BF16),
                jax.ShapeDtypeStruct((2 * cap, width), F32),
            ],
            in_specs=[VMEM] * 9,
            out_specs=[VMEM, VMEM],
            scratch_shapes=[
                pltpu.VMEM((4 * cap, width), BF16),
                pltpu.VMEM((2, 4 * cap, hid), BF16),
            ],
            compiler_params=pltpu.CompilerParams(vmem_limit_bytes=24 * 2**20),
            cost_estimate=pl.CostEstimate(
                flops=32 * cap * width * hid, bytes_accessed=10 * 2**20, transcendentals=0
            ),
            name="expert",
        )(peer, a, b, up, got["u"], down, got["d"], full[:, : 2 * hid], full[:, 2 * hid :])

    def both(a, b):
        return jnp.concatenate([a, b], axis=0)

    def join(own, back):
        done = (own + back.astype(F32)).astype(BF16)
        return done[:cap], done[cap:]

    got, parts, sums, state = {"e0": send[0]}, {}, {}, {}

    def rows_of(k):
        return got["e%d" % (2 * k)], got["e%d" % (2 * k + 1)]

    def run_chunk(k):
        if k not in parts:
            if "full" not in state:
                state["full"] = both(state["pair"], got["b"])
            peer = got["y%d" % k]
            if "last" in state:
                peer = after(peer, state["last"])
            parts[k] = run_expert(peer, *rows_of(k))
            state["last"] = got["E%d" % k] = parts[k][0]
        return parts[k]

    def run_sum(k):
        if k not in sums:
            sums[k] = join(run_chunk(k)[1], got["r%d" % k])
        return sums[k]

    def source(name):
        kind, number = name[0], int(name[1:] or 0)
        if kind == "e":
            return send[number], "expert", number
        if kind == "y":
            return both(*rows_of(number)), "dp", 2
        if kind == "r":
            return run_chunk(number)[0], "dp", 2
        if kind == "o":
            return run_sum(number // 2)[number % 2], "expert", number
        if kind == "a":
            return theirs, "dp", 2
        if kind == "b":
            state["pair"] = both(mine, got["a"])
            return state["pair"], "dp", 1
        return (up if kind == "u" else down), "dp", 1

    for item in ORDER:
        name, _, gates = item.partition(":")
        x, axis, bit = source(name)
        if gates:
            x = after(x, *[got[g] for g in gates.split(",")])
        got[name] = flip(x, axis, bit)
    backs = [run_sum(0)[0]] + [got["o%d" % j] for j in range(1, experts)]

    return pl.pallas_call(
        functools.partial(mix_kernel, cap),
        out_shape=jax.ShapeDtypeStruct((count, width), BF16),
        in_specs=[VMEM] * (2 + experts),
        out_specs=VMEM,
        compiler_params=pltpu.CompilerParams(vmem_limit_bytes=8 * 2**20),
        cost_estimate=pl.CostEstimate(flops=2 * 10**8, bytes_accessed=2 * 10**6, transcendentals=0),
        name="mix",
    )(expert_ids, combine, *backs)


def expert_part(sent_rows, slot_codes, w_up, down_matrix, adapter_input_piece, adapter_output_full):
    language_count = adapter_input_piece.shape[0]
    adapter_rank = adapter_input_piece.shape[1]
    hidden_state = jnp.maximum(
        jnp.dot(sent_rows, w_up, preferred_element_type=jnp.float32), 0.0
    ).astype(jnp.bfloat16)
    input_flattened = adapter_input_piece.reshape(
        language_count * adapter_rank, adapter_input_piece.shape[2]
    )
    reduced_rank = lax.dot_general(
        hidden_state, input_flattened, (((1,), (1,)), ((), ())), preferred_element_type=jnp.float32
    )
    column_position = jnp.arange(language_count * adapter_rank, dtype=jnp.int32) // adapter_rank
    keep_mask = slot_codes[:, None] - 1 == column_position[None, :]
    reduced_rank = jnp.where(keep_mask, reduced_rank, 0.0).astype(jnp.bfloat16)
    output_flattened = adapter_output_full.reshape(
        language_count * adapter_rank, adapter_output_full.shape[2]
    )
    adapter_update = jnp.dot(reduced_rank, output_flattened, preferred_element_type=jnp.float32)
    return jnp.dot(hidden_state, down_matrix, preferred_element_type=jnp.float32) + adapter_update


def build_send(tokens, expert_ids, language, lang_slot, expert_count, capacity):
    tok_count = tokens.shape[0]
    flat_route = jnp.concatenate([expert_ids[:, 0], expert_ids[:, 1]])
    expert_range = jnp.arange(expert_count, dtype=jnp.int32)
    one_hot = (flat_route[:, None] == expert_range[None, :]).astype(jnp.int32)
    before = jnp.cumsum(one_hot, axis=0) - one_hot
    position = jnp.sum(before * one_hot, axis=1)
    slot_of_row = flat_route * capacity + position
    slot_range = jnp.arange(expert_count * capacity, dtype=jnp.int32)
    row_range = jnp.arange(2 * tok_count, dtype=jnp.int32)
    source = jnp.sum(
        jnp.where(slot_of_row[None, :] == slot_range[:, None], row_range[None, :] + 1, 0), axis=1
    )
    filled = source > 0
    token_index = jnp.where(filled, source - 1, 0) % tok_count
    lang_range = jnp.arange(lang_slot.shape[0], dtype=jnp.int32)
    token_slot = jnp.sum(
        jnp.where(language[:, None] == lang_range[None, :], lang_slot[None, :], 0), axis=1
    )
    sent_rows = jnp.where(
        filled[:, None], jnp.take(tokens, token_index, axis=0), jnp.zeros((), tokens.dtype)
    )
    slot_codes = jnp.where(filled, jnp.take(token_slot, token_index) + 1, 0)
    return (
        sent_rows.reshape(expert_count, capacity, -1),
        slot_codes.reshape(expert_count, capacity),
        slot_of_row,
    )


def local(
    tokens,
    expert_ids,
    combine,
    language,
    lang_slot,
    up_weight,
    down_weight,
    adapter_in,
    adapter_out,
):
    tok_count = tokens.shape[0]
    model_width = tokens.shape[1]
    expert_count = lax.axis_size("expert")
    dp_count = lax.axis_size("dp")
    capacity = 3 * tok_count // expert_count
    send_rows, send_codes, slot_of_row = build_send(
        tokens, expert_ids, language, lang_slot, expert_count, capacity
    )
    got_rows, got_codes = (
        lax.all_to_all(send_rows, "expert", split_axis=0, concat_axis=0, tiled=True),
        lax.all_to_all(send_codes, "expert", split_axis=0, concat_axis=0, tiled=True),
    )
    in_part = lax.all_to_all(adapter_in, "dp", split_axis=3, concat_axis=0, tiled=True)
    all_rows, all_codes, out_full = (
        lax.all_gather(got_rows, "dp", axis=0, tiled=True),
        lax.all_gather(got_codes, "dp", axis=0, tiled=True),
        lax.all_gather(adapter_out, "dp", axis=0, tiled=True),
    )
    partial_term = expert_part(
        all_rows.reshape(-1, model_width),
        all_codes.reshape(-1),
        up_weight[0],
        down_weight[0],
        in_part[:, 0],
        out_full[:, 0],
    )
    rounded_term = partial_term.astype(jnp.bfloat16)
    summed = lax.psum_scatter(
        rounded_term.reshape(dp_count, expert_count, capacity, model_width),
        "dp",
        scatter_dimension=0,
        tiled=True,
    ).astype(jnp.float32)
    result_rows = summed.astype(jnp.bfloat16).reshape(expert_count, capacity, model_width)
    returned = lax.all_to_all(result_rows, "expert", split_axis=0, concat_axis=0, tiled=True)
    flat_back = returned.reshape(expert_count * capacity, model_width)
    picked = jnp.take(flat_back, slot_of_row, axis=0).astype(jnp.float32)
    mixed_out = combine[:, 0:1] * picked[:tok_count] + combine[:, 1:2] * picked[tok_count:]
    return mixed_out.astype(jnp.bfloat16)


def solution(mesh):
    placed = (
        P(("expert", "dp"), None),
        P(("expert", "dp"), None),
        P(("expert", "dp"), None),
        P(("expert", "dp")),
        P(),
        P("expert", None, "dp"),
        P("expert", "dp", None),
        P("dp", "expert", None, None),
        P("dp", "expert", None, None),
    )
    pairs = mesh.shape["dp"] == 4 and mesh.shape["expert"] == 8
    body = local_pairs if pairs else local
    return jax.shard_map(
        body, mesh=mesh, in_specs=placed, out_specs=P(("expert", "dp"), None), check_vma=False
    )
```
